256 devices in a mesh: rep: 32 (over z, y), fsdp: 8 (over x, core).
Axes of the slice: x: 4, y: 4, z: 8, core: 2. Of those that a mesh axis runs over, the one named last changes fastest.
Arguments:
- local_params: bfloat16 [32, 256, 8192], P('rep', 'fsdp'), may hold values from -120 to 120
- base_params: bfloat16 [256, 8192], P('fsdp'), may hold values from -4 to 4
- momentum: float32 [256, 8192], P('fsdp'), may hold values from -4 to 4
Outputs:
- new_base: bfloat16 [256, 8192], replicated
- new_momentum: float32 [256, 8192], P('fsdp')
The draws below stay inside these ranges and needn't reach their ends.
All inputs are finite; a program needn't handle non-finite values.
Results may differ from the reference program's by a relative error of at most 0.015.
Values may be sent and summed in bfloat16 or wider, within the bound.
No kernel may reach another device: no remote copies, remote signals or barrier semaphores. Data moves between devices by JAX's collectives and lax.ppermute only.
A program may use at most 64 MiB of HBM per device.

```python
import jax
import jax.numpy as jnp
from jax import lax

D = 8192
BLOCK = 32
ROWS = 256
REPLICAS = 32


def shared_fragment(key):
    return jnp.clip(jax.random.normal(key, (ROWS, D), jnp.float32), -4.0, 4.0)


def draw_base_params(key, part):
    return shared_fragment(key).astype(jnp.bfloat16)


def draw_local_params(key, part):
    fragment = shared_fragment(key)
    key = jax.random.fold_in(key, 11)
    key_noise = jax.random.fold_in(key, 0)
    key_rows = jax.random.fold_in(key, 1)
    key_cols = jax.random.fold_in(key, 2)
    key_elem = jax.random.fold_in(key, 4)
    row_scale = jnp.exp(jax.random.uniform(key_rows, (REPLICAS, ROWS, 1), jnp.float32, jnp.log(0.3), jnp.log(3.0)))
    col_scale = jnp.exp(jax.random.uniform(key_cols, (1, 1, D), jnp.float32, jnp.log(0.3), jnp.log(3.0)))
    elem_scale = jnp.exp(jax.random.uniform(key_elem, (REPLICAS, ROWS, D), jnp.float32, jnp.log(0.3), jnp.log(3.0)))
    noise_vals = jnp.clip(jax.random.normal(key_noise, (REPLICAS, ROWS, D), jnp.float32), -4.0, 4.0) * elem_scale
    return (fragment[None, :, :] - noise_vals * row_scale * col_scale).astype(jnp.bfloat16)


def block_levels(own_key, extent, pieces, least, top_value):
    def one(axis_at, blocks):
        draws = jax.random.uniform(jax.random.fold_in(jax.random.fold_in(own_key, 6), axis_at), (blocks,), jnp.float32, least / len(pieces), top_value / len(pieces))
        return jnp.repeat(jnp.exp(draws), extent[axis_at] // blocks).reshape((-1,) + (1,) * (len(extent) - axis_at - 1))

    factor_of = one(*pieces[0])
    for cut in pieces[1:]:
        factor_of = factor_of * one(*cut)
    return factor_of


def gaussian(rng, dims, spread, limit, cuts=(), held_as=jnp.bfloat16):
    level = block_levels(rng, dims, cuts, -0.22, 0.18) if cuts else 1.0
    array = jax.random.normal(rng, dims, jnp.float32) * spread * level
    return jnp.minimum(jnp.maximum(array, -limit), limit).astype(held_as)


def setup_inputs(seed: int = 0) -> dict:
    key_of = jax.random.split(jax.random.key(seed), 4)
    return {
        "local_params": draw_local_params(jax.random.fold_in(key_of[3], 71), 0),
        "base_params": draw_base_params(jax.random.fold_in(key_of[3], 71), 0),
        "momentum": gaussian(key_of[2], (ROWS, D), 0.3, 4.0, ((0, 8),), jnp.float32),
    }


floor_value = 0.5
spread_ratio = 3.0
code_peak = 6.0
outer_rate = 0.7
momentum_coef = 0.9

def encode(local_rows, base_rows):
    pseudo_grad = base_rows.astype(jnp.float32) - local_rows.astype(jnp.float32)
    blocks = pseudo_grad.reshape(pseudo_grad.shape[0], pseudo_grad.shape[1] // BLOCK, BLOCK)
    mean_square = lax.optimization_barrier(jnp.mean(blocks * blocks, axis=2))
    block_scale = lax.optimization_barrier((jnp.maximum(jnp.sqrt(mean_square), floor_value) / spread_ratio).astype(jnp.bfloat16))
    ratios = blocks / block_scale.astype(jnp.float32)[:, :, None]
    quant_codes = lax.optimization_barrier(jnp.clip(ratios, -code_peak, code_peak).astype(jnp.bfloat16))
    return (quant_codes, block_scale)

def dequantize(quant_codes, block_scale):
    values = quant_codes.astype(jnp.float32) * block_scale.astype(jnp.float32)[:, :, None]
    return values.reshape(values.shape[0], values.shape[1] * values.shape[2])

def reference(local_params, base_params, momentum):

    def add_replica(summed, local_rows):
        quant_codes, block_scale = encode(local_rows, base_params)
        return (summed + dequantize(quant_codes, block_scale), None)
    summed, _ = lax.scan(add_replica, jnp.zeros(base_params.shape, jnp.float32), local_params)
    average = summed / REPLICAS
    new_momentum = momentum_coef * momentum + average
    new_base = (base_params.astype(jnp.float32) - outer_rate * (average + momentum_coef * new_momentum)).astype(jnp.bfloat16)
    return (new_base, new_momentum)
```

```python
import jax
import jax.numpy as jnp
from jax import lax
from jax.experimental import pallas as pl
from jax.experimental.pallas import tpu as pltpu
from jax.sharding import Mesh, PartitionSpec as P

BLOCK = 32

floor_value = 0.5
spread_ratio = 3.0
code_peak = 6.0
outer_rate = 0.7
momentum_coef = 0.9

ROWS = 32
HALF = 16
COLS = 8192
PIECES = 4
WIDE = COLS // PIECES
LANES = 128


def encode_kernel(local_ref, base_ref, out_ref):
    lane = lax.broadcasted_iota(jnp.int32, (LANES, LANES), 0) // BLOCK
    lane_t = lax.broadcasted_iota(jnp.int32, (LANES, LANES), 1) // BLOCK
    same_block = jnp.where(lane == lane_t, 1.0 / BLOCK, 0.0).astype(jnp.float32)
    for half in range(2):
        for piece in range(PIECES):
            rows = pl.ds(half * HALF, HALF)
            cols = pl.ds(piece * WIDE, WIDE)
            grad = base_ref[rows, cols].astype(jnp.float32) - local_ref[0, rows, cols].astype(
                jnp.float32
            )
            tall = jnp.concatenate(
                [grad[:, k * LANES : (k + 1) * LANES] for k in range(WIDE // LANES)], axis=0
            )
            mean_square = jnp.dot(
                tall * tall,
                same_block,
                precision=lax.Precision.HIGHEST,
                preferred_element_type=jnp.float32,
            )
            scale = (jnp.maximum(jnp.sqrt(mean_square), floor_value) / spread_ratio).astype(
                jnp.bfloat16
            )
            limit = code_peak * scale.astype(jnp.float32)
            decoded = jnp.clip(tall, -limit, limit).astype(jnp.bfloat16)
            for k in range(WIDE // LANES):
                out_ref[half * PIECES + piece, :, k * LANES : (k + 1) * LANES] = decoded[
                    k * HALF : (k + 1) * HALF
                ]


def encode(local_params, base_rows):
    return pl.pallas_call(
        encode_kernel,
        out_shape=jax.ShapeDtypeStruct((2 * PIECES, HALF, WIDE), jnp.bfloat16),
        name="encode",
    )(local_params, base_rows)


def update_kernel(average_ref, base_ref, momentum_ref, first_ref, second_ref, new_momentum_ref):
    for half, new_base_ref in ((0, first_ref), (1, second_ref)):
        for piece in range(PIECES):
            rows = pl.ds(half * HALF, HALF)
            cols = pl.ds(piece * WIDE, WIDE)
            average = average_ref[half * PIECES + piece].astype(jnp.float32)
            new_momentum = momentum_coef * momentum_ref[rows, cols] + average
            new_momentum_ref[rows, cols] = new_momentum
            new_base_ref[:, cols] = (
                base_ref[rows, cols].astype(jnp.float32)
                - outer_rate * (average + momentum_coef * new_momentum)
            ).astype(jnp.bfloat16)


def outer_update(average, base_rows, momentum):
    part = jax.ShapeDtypeStruct((HALF, COLS), jnp.bfloat16)
    return pl.pallas_call(
        update_kernel,
        out_shape=(part, part, jax.ShapeDtypeStruct((ROWS, COLS), jnp.float32)),
        name="outer_update",
    )(average, base_rows, momentum)


def assemble_kernel(place_ref, *refs):
    parts, out_ref, sems = refs[:16], refs[16], refs[17]
    copies = []
    for k in range(16):
        start = pl.multiple_of(place_ref[k] * HALF, HALF)
        copies.append(
            pltpu.make_async_copy(parts[k], out_ref.at[pl.ds(start, HALF), :], sems.at[k])
        )
    for copy in copies:
        copy.start()
    for copy in copies:
        copy.wait()


def assemble(places, parts):
    return pl.pallas_call(
        assemble_kernel,
        out_shape=jax.ShapeDtypeStruct((16 * HALF, COLS), jnp.bfloat16),
        in_specs=[pl.BlockSpec(memory_space=pltpu.SMEM)]
        + [pl.BlockSpec(memory_space=pl.ANY)] * 16,
        out_specs=pl.BlockSpec(memory_space=pl.ANY),
        scratch_shapes=[pltpu.SemaphoreType.DMA((16,))],
        name="assemble",
    )(places, *parts)


def ring(n, step):
    return [(i, (i + step) % n) for i in range(n)]


def shards(local_params, base_params, momentum):
    decoded = encode(local_params, base_params)

    near = ("zl", "y")
    received = lax.all_to_all(decoded, near, 0, 0, tiled=True)
    partial = jnp.sum(received.astype(jnp.float32), axis=0).astype(jnp.bfloat16)

    others = [lax.ppermute(partial, "zh", ring(4, k)) for k in (1, 2, 3)]
    one, two, three = [value.astype(jnp.float32) for value in others]
    total = (partial.astype(jnp.float32) + two) + (one + three)
    average = (total / 32).astype(jnp.bfloat16)

    gathered = lax.all_to_all(
        jnp.broadcast_to(average[None], (8,) + average.shape), near, 0, 0, tiled=True
    )

    first, second, new_momentum = outer_update(gathered, base_params, momentum)

    left = [lax.ppermute(half, "x", ring(4, 1)) for half in (first, second)]
    right = [lax.ppermute(half, "x", ring(4, 3)) for half in (second, first)]
    far = [lax.ppermute(left[0], "x", ring(4, 1)), lax.ppermute(right[0], "x", ring(4, 3))]
    mine = [first, second, left[0], left[1], right[1], right[0], far[0], far[1]]
    theirs = [lax.ppermute(part, "core", ring(2, 1)) for part in mine]

    x, core = lax.axis_index("x"), lax.axis_index("core")
    at = [x, x, (x + 3) % 4, (x + 3) % 4, (x + 1) % 4, (x + 1) % 4, (x + 2) % 4, (x + 2) % 4]
    places = [(at[k] * 2 + c) * 2 + k % 2 for c in (core, 1 - core) for k in range(8)]
    new_base = assemble(jnp.stack(places).astype(jnp.int32), mine + theirs)
    return (new_base, new_momentum)


def solution(mesh):
    fine = Mesh(mesh.devices.reshape(4, 2, 4, 4, 2), ("zh", "zl", "y", "x", "core"))
    rep, fsdp = ("zh", "zl", "y"), ("x", "core")
    in_specs = (P(rep, fsdp, None), P(fsdp, None), P(fsdp, None))
    out_specs = (P(), P(fsdp, None))
    return jax.shard_map(shards, mesh=fine, in_specs=in_specs, out_specs=out_specs, check_vma=False)
```

```python
import jax
import jax.numpy as jnp
from jax import lax
from jax.experimental import pallas as pl
from jax.experimental.pallas import tpu as pltpu
from jax.sharding import Mesh, PartitionSpec as P

BLOCK = 32

floor_value = 0.5
spread_ratio = 3.0
code_peak = 6.0
outer_rate = 0.7
momentum_coef = 0.9

ROWS = 32
HALF = 16
COLS = 8192
PIECES = 4
WIDE = COLS // PIECES
LANES = 128

SMALL = pltpu.CompilerParams(vmem_limit_bytes=16 << 20)


def encode_kernel(local_ref, base_ref, out_ref):
    lane = lax.broadcasted_iota(jnp.int32, (LANES, LANES), 0) // BLOCK
    lane_t = lax.broadcasted_iota(jnp.int32, (LANES, LANES), 1) // BLOCK
    same_block = jnp.where(lane == lane_t, 1.0 / BLOCK, 0.0).astype(jnp.float32)
    for half in range(2):
        for piece in range(PIECES):
            rows = pl.ds(half * HALF, HALF)
            cols = pl.ds(piece * WIDE, WIDE)
            grad = base_ref[rows, cols].astype(jnp.float32) - local_ref[0, rows, cols].astype(
                jnp.float32
            )
            tall = jnp.concatenate(
                [grad[:, k * LANES : (k + 1) * LANES] for k in range(WIDE // LANES)], axis=0
            )
            mean_square = jnp.dot(
                tall * tall,
                same_block,
                precision=lax.Precision.HIGHEST,
                preferred_element_type=jnp.float32,
            )
            scale = (jnp.maximum(jnp.sqrt(mean_square), floor_value) / spread_ratio).astype(
                jnp.bfloat16
            )
            limit = code_peak * scale.astype(jnp.float32)
            decoded = jnp.clip(tall, -limit, limit).astype(jnp.bfloat16)
            for k in range(WIDE // LANES):
                out_ref[half * PIECES + piece, :, k * LANES : (k + 1) * LANES] = decoded[
                    k * HALF : (k + 1) * HALF
                ]


def in_vmem(value):
    return pltpu.with_memory_space_constraint(value, pltpu.VMEM)


def encode(local_params, base_rows):
    return pl.pallas_call(
        encode_kernel,
        out_shape=pltpu.VMEM((2 * PIECES, HALF, WIDE), jnp.bfloat16),
        compiler_params=SMALL,
        name="encode",
    )(local_params, base_rows)


def update_kernel(average_ref, base_ref, momentum_ref, first_ref, second_ref, new_momentum_ref):
    for half, new_base_ref in ((0, first_ref), (1, second_ref)):
        for piece in range(PIECES):
            rows = pl.ds(half * HALF, HALF)
            cols = pl.ds(piece * WIDE, WIDE)
            average = average_ref[half * PIECES + piece].astype(jnp.float32)
            new_momentum = momentum_coef * momentum_ref[rows, cols] + average
            new_momentum_ref[rows, cols] = new_momentum
            new_base_ref[:, cols] = (
                base_ref[rows, cols].astype(jnp.float32)
                - outer_rate * (average + momentum_coef * new_momentum)
            ).astype(jnp.bfloat16)


def outer_update(average, base_rows, momentum):
    part = pltpu.VMEM((HALF, COLS), jnp.bfloat16)
    return pl.pallas_call(
        update_kernel,
        out_shape=(part, part, jax.ShapeDtypeStruct((ROWS, COLS), jnp.float32)),
        compiler_params=SMALL,
        name="outer_update",
    )(in_vmem(average), base_rows, momentum)


def assemble_kernel(place_ref, *refs):
    parts, out_ref, sems = refs[:16], refs[16], refs[17]
    copies = []
    for k in range(16):
        start = pl.multiple_of(place_ref[k] * HALF, HALF)
        copies.append(
            pltpu.make_async_copy(parts[k], out_ref.at[pl.ds(start, HALF), :], sems.at[k])
        )
    for copy in copies:
        copy.start()
    for copy in copies:
        copy.wait()


def assemble(places, parts):
    return pl.pallas_call(
        assemble_kernel,
        out_shape=jax.ShapeDtypeStruct((16 * HALF, COLS), jnp.bfloat16),
        in_specs=[pl.BlockSpec(memory_space=pltpu.SMEM)]
        + [pl.BlockSpec(memory_space=pltpu.VMEM)] * 16,
        out_specs=pl.BlockSpec(memory_space=pl.ANY),
        scratch_shapes=[pltpu.SemaphoreType.DMA((16,))],
        compiler_params=SMALL,
        name="assemble",
    )(places, *[in_vmem(part) for part in parts])


def ring(n, step):
    return [(i, (i + step) % n) for i in range(n)]


def shards(local_params, base_params, momentum):
    decoded = encode(local_params, base_params)

    near = ("zl", "y")
    received = lax.all_to_all(decoded, near, 0, 0, tiled=True)
    partial = jnp.sum(received.astype(jnp.float32), axis=0).astype(jnp.bfloat16)

    others = [lax.ppermute(partial, "zh", ring(4, k)) for k in (1, 2, 3)]
    one, two, three = [value.astype(jnp.float32) for value in others]
    total = (partial.astype(jnp.float32) + two) + (one + three)
    average = (total / 32).astype(jnp.bfloat16)

    gathered = lax.all_to_all(
        jnp.broadcast_to(average[None], (8,) + average.shape), near, 0, 0, tiled=True
    )

    first, second, new_momentum = outer_update(gathered, base_params, momentum)

    left = [lax.ppermute(half, "x", ring(4, 1)) for half in (first, second)]
    right = [lax.ppermute(half, "x", ring(4, 3)) for half in (second, first)]
    far = [lax.ppermute(left[0], "x", ring(4, 1)), lax.ppermute(right[0], "x", ring(4, 3))]
    mine = [first, second, left[0], left[1], right[1], right[0], far[0], far[1]]
    theirs = [lax.ppermute(part, "core", ring(2, 1)) for part in mine]

    x, core = lax.axis_index("x"), lax.axis_index("core")
    at = [x, x, (x + 3) % 4, (x + 3) % 4, (x + 1) % 4, (x + 1) % 4, (x + 2) % 4, (x + 2) % 4]
    places = [(at[k] * 2 + c) * 2 + k % 2 for c in (core, 1 - core) for k in range(8)]
    new_base = assemble(jnp.stack(places).astype(jnp.int32), mine + theirs)
    return (new_base, new_momentum)


def solution(mesh):
    fine = Mesh(mesh.devices.reshape(4, 2, 4, 4, 2), ("zh", "zl", "y", "x", "core"))
    rep, fsdp = ("zh", "zl", "y"), ("x", "core")
    in_specs = (P(rep, fsdp, None), P(fsdp, None), P(fsdp, None))
    out_specs = (P(), P(fsdp, None))
    return jax.shard_map(shards, mesh=fine, in_specs=in_specs, out_specs=out_specs, check_vma=False)
```

```python
import functools

import jax
import jax.numpy as jnp
from jax import lax
from jax.experimental import pallas as pl
from jax.experimental.pallas import tpu as pltpu
from jax.sharding import Mesh, PartitionSpec as P

BLOCK = 32

floor_value = 0.5
spread_ratio = 3.0
code_peak = 6.0
outer_rate = 0.7
momentum_coef = 0.9

ROWS = 32
HALF = 16
COLS = 8192
PIECES = 4
WIDE = COLS // PIECES
LANES = 128

SMALL = pltpu.CompilerParams(vmem_limit_bytes=16 << 20)


def encode_kernel(local_hbm, base_hbm, out_ref, local_ref, base_ref, sems):
    copies = []
    for half in range(2):
        rows = pl.ds(half * HALF, HALF)
        copies.append(
            (
                pltpu.make_async_copy(
                    local_hbm.at[0, rows, :], local_ref.at[half], sems.at[0, half]
                ),
                pltpu.make_async_copy(base_hbm.at[rows, :], base_ref.at[half], sems.at[1, half]),
            )
        )
    for pair in copies:
        for copy in pair:
            copy.start()
    block = lax.broadcasted_iota(jnp.int32, (LANES, LANES), 0) // BLOCK
    block_t = lax.broadcasted_iota(jnp.int32, (LANES, LANES), 1) // BLOCK
    same_block = jnp.where(block == block_t, 1.0 / BLOCK, 0.0).astype(jnp.float32)
    for k in range(2 * PIECES):
        half, piece = k // PIECES, k % PIECES
        if piece == 0:
            for copy in copies[half]:
                copy.wait()
        cols = pl.ds(piece * WIDE, WIDE)
        grad = base_ref[half, :, cols].astype(jnp.float32) - local_ref[half, :, cols].astype(
            jnp.float32
        )
        tall = jnp.concatenate(
            [grad[:, i * LANES : (i + 1) * LANES] for i in range(WIDE // LANES)], axis=0
        )
        mean_square = jnp.dot(
            tall * tall,
            same_block,
            precision=lax.Precision.HIGHEST,
            preferred_element_type=jnp.float32,
        )
        scale = (jnp.maximum(jnp.sqrt(mean_square), floor_value) / spread_ratio).astype(
            jnp.bfloat16
        )
        limit = code_peak * scale.astype(jnp.float32)
        decoded = jnp.clip(tall, -limit, limit).astype(jnp.bfloat16)
        for i in range(WIDE // LANES):
            out_ref[k, :, i * LANES : (i + 1) * LANES] = decoded[i * HALF : (i + 1) * HALF]


def in_vmem(value):
    return pltpu.with_memory_space_constraint(value, pltpu.VMEM)


def in_hbm(value):
    return pltpu.with_memory_space_constraint(value, pltpu.HBM)


def encode(local_params, base_rows):
    halves = (2, HALF, COLS)
    return pl.pallas_call(
        encode_kernel,
        out_shape=pltpu.VMEM((2 * PIECES, HALF, WIDE), jnp.bfloat16),
        in_specs=[pl.BlockSpec(memory_space=pltpu.HBM)] * 2,
        scratch_shapes=[
            pltpu.VMEM(halves, jnp.bfloat16),
            pltpu.VMEM(halves, jnp.bfloat16),
            pltpu.SemaphoreType.DMA((2, 2)),
        ],
        compiler_params=SMALL,
        name="encode",
    )(in_hbm(local_params), in_hbm(base_rows))


def update_kernel(
    average_ref, base_ref, momentum_ref, first_ref, second_ref, own_ref, new_momentum_ref
):
    for half, new_base_ref in ((0, first_ref), (1, second_ref)):
        for piece in range(PIECES):
            rows = pl.ds(half * HALF, HALF)
            cols = pl.ds(piece * WIDE, WIDE)
            average = average_ref[half * PIECES + piece].astype(jnp.float32)
            new_momentum = momentum_coef * momentum_ref[rows, cols] + average
            new_momentum_ref[rows, cols] = new_momentum
            new_base = (
                base_ref[rows, cols].astype(jnp.float32)
                - outer_rate * (average + momentum_coef * new_momentum)
            ).astype(jnp.bfloat16)
            new_base_ref[:, cols] = new_base
            own_ref[rows, cols] = new_base


def outer_update(average, base_rows, momentum):
    part = pltpu.VMEM((HALF, COLS), jnp.bfloat16)
    own = pltpu.VMEM((ROWS, COLS), jnp.bfloat16)
    return pl.pallas_call(
        update_kernel,
        out_shape=(part, part, own, jax.ShapeDtypeStruct((ROWS, COLS), jnp.float32)),
        compiler_params=SMALL,
        name="outer_update",
    )(in_vmem(average), base_rows, momentum)


def join_kernel(one_ref, two_ref, out_ref):
    out_ref[pl.ds(0, HALF), :] = one_ref[...]
    out_ref[pl.ds(HALF, HALF), :] = two_ref[...]


def join(one, two):
    return pl.pallas_call(
        join_kernel,
        out_shape=pltpu.VMEM((ROWS, COLS), jnp.bfloat16),
        compiler_params=SMALL,
        name="join",
    )(in_vmem(one), in_vmem(two))


def place_kernel(count, place_ref, *refs):
    parts, out_ref, sems = refs[:count], refs[-2], refs[-1]
    copies = []
    for ref in parts:
        for k in range(ref.shape[0] // HALF):
            start = pl.multiple_of(place_ref[len(copies)] * HALF, HALF)
            copies.append(
                pltpu.make_async_copy(
                    ref.at[pl.ds(k * HALF, HALF), :],
                    out_ref.at[pl.ds(start, HALF), :],
                    sems.at[len(copies)],
                )
            )
    for copy in copies:
        copy.start()
    for copy in copies:
        copy.wait()


def place(rows, parts, whole=None):
    count = len(parts)
    total = sum(part.shape[0] for part in parts) // HALF
    keep = [] if whole is None else [whole]
    hbm = pl.BlockSpec(memory_space=pltpu.HBM)
    return pl.pallas_call(
        functools.partial(place_kernel, count),
        out_shape=pltpu.HBM((16 * HALF, COLS), jnp.bfloat16),
        in_specs=[pl.BlockSpec(memory_space=pltpu.SMEM)]
        + [pl.BlockSpec(memory_space=pltpu.VMEM)] * count
        + [hbm] * len(keep),
        out_specs=hbm,
        scratch_shapes=[pltpu.SemaphoreType.DMA((total,))],
        input_output_aliases={count + 1: 0} if keep else {},
        compiler_params=SMALL,
        cost_estimate=pl.CostEstimate(
            flops=0, transcendentals=0, bytes_accessed=total * HALF * COLS * 4
        ),
        name="place",
    )(
        jnp.stack(rows).astype(jnp.int32),
        *[in_vmem(part) for part in parts],
        *[in_hbm(w) for w in keep],
    )


def ring(n, step):
    return [(i, (i + step) % n) for i in range(n)]


def shards(local_params, base_params, momentum):
    decoded = encode(local_params, base_params)

    near = ("zl", "y")
    received = lax.all_to_all(decoded, near, 0, 0, tiled=True)
    partial = jnp.sum(received.astype(jnp.float32), axis=0).astype(jnp.bfloat16)

    others = [lax.ppermute(partial, "zh", ring(4, k)) for k in (1, 2, 3)]
    one, two, three = [value.astype(jnp.float32) for value in others]
    total = (partial.astype(jnp.float32) + two) + (one + three)
    average = (total / 32).astype(jnp.bfloat16)

    gathered = lax.all_to_all(
        jnp.broadcast_to(average[None], (8,) + average.shape), near, 0, 0, tiled=True
    )

    first, second, own, new_momentum = outer_update(gathered, base_params, momentum)

    def swap(part):
        return lax.ppermute(part, "core", ring(2, 1))

    x, core = lax.axis_index("x"), lax.axis_index("core")

    def rows(step, c):
        return [(((x + step) % 4) * 2 + c) * 2 + half for half in range(2)]

    left = [lax.ppermute(half, "x", ring(4, 1)) for half in (first, second)]
    right = [lax.ppermute(half, "x", ring(4, 3)) for half in (second, first)]
    far = [lax.ppermute(left[0], "x", ring(4, 1)), lax.ppermute(right[0], "x", ring(4, 3))]

    from_left = join(left[0], left[1])
    from_right = join(right[1], right[0])
    from_far = join(far[0], far[1])
    near = [own, from_left, from_right]
    near_steps, far_step = (0, 3, 1), 2
    new_base = place(
        [r for step in near_steps for r in rows(step, core)]
        + [r for step in near_steps for r in rows(step, 1 - core)]
        + rows(far_step, core),
        near + [swap(part) for part in near] + [from_far],
    )
    new_base = place(rows(far_step, 1 - core), [swap(from_far)], new_base)
    return (new_base, new_momentum)


def solution(mesh):
    fine = Mesh(mesh.devices.reshape(4, 2, 4, 4, 2), ("zh", "zl", "y", "x", "core"))
    rep, fsdp = ("zh", "zl", "y"), ("x", "core")
    in_specs = (P(rep, fsdp, None), P(fsdp, None), P(fsdp, None))
    out_specs = (P(), P(fsdp, None))
    return jax.shard_map(shards, mesh=fine, in_specs=in_specs, out_specs=out_specs, check_vma=False)
```

```python
import functools

import jax
import jax.numpy as jnp
from jax import lax
from jax.experimental import pallas as pl
from jax.experimental.pallas import tpu as pltpu
from jax.sharding import Mesh, PartitionSpec as P

BLOCK = 32

floor_value = 0.5
spread_ratio = 3.0
code_peak = 6.0
outer_rate = 0.7
momentum_coef = 0.9

ROWS = 32
HALF = 16
COLS = 8192
PIECES = 4
WIDE = COLS // PIECES
LANES = 128

SMALL = pltpu.CompilerParams(vmem_limit_bytes=8 << 20)
TINY = pltpu.CompilerParams(vmem_limit_bytes=4 << 20)


def encode_kernel(local_hbm, base_hbm, out_ref, local_ref, base_ref, sems):
    copies = []
    for half in range(2):
        rows = pl.ds(half * HALF, HALF)
        copies.append(
            (
                pltpu.make_async_copy(
                    local_hbm.at[0, rows, :], local_ref.at[half], sems.at[0, half]
                ),
                pltpu.make_async_copy(base_hbm.at[rows, :], base_ref.at[half], sems.at[1, half]),
            )
        )
    for pair in copies:
        for copy in pair:
            copy.start()
    block = lax.broadcasted_iota(jnp.int32, (LANES, LANES), 0) // BLOCK
    block_t = lax.broadcasted_iota(jnp.int32, (LANES, LANES), 1) // BLOCK
    same_block = jnp.where(block == block_t, 1.0 / BLOCK, 0.0).astype(jnp.float32)
    for k in range(2 * PIECES):
        half, piece = k // PIECES, k % PIECES
        if piece == 0:
            for copy in copies[half]:
                copy.wait()
        cols = pl.ds(piece * WIDE, WIDE)
        grad = base_ref[half, :, cols].astype(jnp.float32) - local_ref[half, :, cols].astype(
            jnp.float32
        )
        tall = jnp.concatenate(
            [grad[:, i * LANES : (i + 1) * LANES] for i in range(WIDE // LANES)], axis=0
        )
        mean_square = jnp.dot(
            tall * tall,
            same_block,
            precision=lax.Precision.HIGHEST,
            preferred_element_type=jnp.float32,
        )
        floored = jnp.maximum(mean_square, floor_value * floor_value)
        scale = (floored * lax.rsqrt(floored) * (1.0 / spread_ratio)).astype(jnp.bfloat16)
        limit = code_peak * scale.astype(jnp.float32)
        decoded = jnp.clip(tall, -limit, limit).astype(jnp.bfloat16)
        for i in range(WIDE // LANES):
            out_ref[k, :, i * LANES : (i + 1) * LANES] = decoded[i * HALF : (i + 1) * HALF]


def in_vmem(value):
    return pltpu.with_memory_space_constraint(value, pltpu.VMEM)


def in_hbm(value):
    return pltpu.with_memory_space_constraint(value, pltpu.HBM)


def encode(local_params, base_rows):
    halves = (2, HALF, COLS)
    return pl.pallas_call(
        encode_kernel,
        out_shape=pltpu.VMEM((2 * PIECES, HALF, WIDE), jnp.bfloat16),
        in_specs=[pl.BlockSpec(memory_space=pltpu.HBM)] * 2,
        scratch_shapes=[
            pltpu.VMEM(halves, jnp.bfloat16),
            pltpu.VMEM(halves, jnp.bfloat16),
            pltpu.SemaphoreType.DMA((2, 2)),
        ],
        compiler_params=SMALL,
        name="encode",
    )(in_hbm(local_params), in_hbm(base_rows))


def pieces():
    for half in range(2):
        for piece in range(PIECES):
            rows, cols = pl.ds(half * HALF, HALF), pl.ds(piece * WIDE, WIDE)
            yield half, half * PIECES + piece, rows, cols


def step_momentum(average, momentum):
    return momentum_coef * momentum + average


def base_kernel(average_ref, base_ref, momentum_ref, *new_base_refs):
    for half, k, rows, cols in pieces():
        average = average_ref[k].astype(jnp.float32)
        new_momentum = step_momentum(average, momentum_ref[rows, cols])
        new_base_refs[half][:, cols] = (
            base_ref[rows, cols].astype(jnp.float32)
            - outer_rate * (average + momentum_coef * new_momentum)
        ).astype(jnp.bfloat16)


def update_base(average, base_rows, momentum):
    part = pltpu.VMEM((HALF, COLS), jnp.bfloat16)
    return pl.pallas_call(
        base_kernel,
        out_shape=(part, part),
        compiler_params=SMALL,
        name="update_base",
    )(in_vmem(average), base_rows, momentum)


def momentum_kernel(average_ref, momentum_hbm, new_hbm, momentum_ref, new_ref, sems):
    reads, writes = [], []
    for half in range(2):
        rows = pl.ds(half * HALF, HALF)
        reads.append(
            pltpu.make_async_copy(momentum_hbm.at[rows, :], momentum_ref.at[half], sems.at[0, half])
        )
        writes.append(pltpu.make_async_copy(new_ref.at[half], new_hbm.at[rows, :], sems.at[1, half]))
    for copy in reads:
        copy.start()
    for half in range(2):
        reads[half].wait()
        for piece in range(PIECES):
            cols = pl.ds(piece * WIDE, WIDE)
            new_ref[half, :, cols] = step_momentum(
                average_ref[half * PIECES + piece].astype(jnp.float32), momentum_ref[half, :, cols]
            )
        writes[half].start()
    for copy in writes:
        copy.wait()


def update_momentum(average, momentum):
    hbm = pl.BlockSpec(memory_space=pltpu.HBM)
    return pl.pallas_call(
        momentum_kernel,
        out_shape=pltpu.HBM((ROWS, COLS), jnp.float32),
        in_specs=[pl.BlockSpec(memory_space=pltpu.VMEM), hbm],
        out_specs=hbm,
        scratch_shapes=[
            pltpu.VMEM((2, HALF, COLS), jnp.float32),
            pltpu.VMEM((2, HALF, COLS), jnp.float32),
            pltpu.SemaphoreType.DMA((2, 2)),
        ],
        compiler_params=SMALL,
        name="update_momentum",
    )(in_vmem(average), in_hbm(momentum))


def after_kernel(*refs):
    pass


def after(part, ready):
    vmem, hbm = pl.BlockSpec(memory_space=pltpu.VMEM), pl.BlockSpec(memory_space=pltpu.HBM)
    return pl.pallas_call(
        after_kernel,
        out_shape=(pltpu.VMEM(part.shape, part.dtype), pltpu.HBM(ready.shape, ready.dtype)),
        in_specs=[vmem, hbm],
        out_specs=(vmem, hbm),
        input_output_aliases={0: 0, 1: 1},
        compiler_params=TINY,
        name="after",
    )(in_vmem(part), in_hbm(ready))


def join_kernel(one_ref, two_ref, out_ref):
    out_ref[pl.ds(0, HALF), :] = one_ref[...]
    out_ref[pl.ds(HALF, HALF), :] = two_ref[...]


def join(one, two):
    return pl.pallas_call(
        join_kernel,
        out_shape=pltpu.VMEM((ROWS, COLS), jnp.bfloat16),
        compiler_params=TINY,
        name="join",
    )(in_vmem(one), in_vmem(two))


def join_after_kernel(one_ref, two_ref, *refs):
    join_kernel(one_ref, two_ref, refs[len(refs) // 2])


def join_after(one, two, *ready):
    vmem, hbm = pl.BlockSpec(memory_space=pltpu.VMEM), pl.BlockSpec(memory_space=pltpu.HBM)
    count = len(ready)
    return pl.pallas_call(
        join_after_kernel,
        out_shape=(pltpu.VMEM((ROWS, COLS), jnp.bfloat16),)
        + tuple(pltpu.HBM(array.shape, array.dtype) for array in ready),
        in_specs=[vmem, vmem] + [hbm] * count,
        out_specs=(vmem,) + (hbm,) * count,
        input_output_aliases={2 + k: 1 + k for k in range(count)},
        compiler_params=TINY,
        name="join_after",
    )(in_vmem(one), in_vmem(two), *[in_hbm(array) for array in ready])


def place_kernel(steps, spot_ref, *refs):
    parts, out_ref, sems = refs[: len(steps)], refs[-2], refs[-1]
    copies = []
    for k, (ref, (step, other, half)) in enumerate(zip(parts, steps)):
        x, core = lax.rem(spot_ref[0] + step, 4), lax.rem(spot_ref[1] + other, 2)
        start = pl.multiple_of((x * 2 + core) * ROWS + half * HALF, HALF)
        copies.append(
            pltpu.make_async_copy(ref, out_ref.at[pl.ds(start, ref.shape[0]), :], sems.at[k])
        )
    for copy in copies:
        copy.start()
    for copy in copies:
        copy.wait()


def place(spot, parts, whole=None):
    steps, count = tuple(parts), len(parts)
    keep = [] if whole is None else [whole]
    hbm = pl.BlockSpec(memory_space=pltpu.HBM)
    return pl.pallas_call(
        functools.partial(place_kernel, steps),
        out_shape=pltpu.HBM((8 * ROWS, COLS), jnp.bfloat16),
        in_specs=[pl.BlockSpec(memory_space=pltpu.SMEM)]
        + [pl.BlockSpec(memory_space=pltpu.VMEM)] * count
        + [hbm] * len(keep),
        out_specs=hbm,
        scratch_shapes=[pltpu.SemaphoreType.DMA((count,))],
        input_output_aliases={count + 1: 0} if keep else {},
        compiler_params=TINY,
        cost_estimate=pl.CostEstimate(
            flops=0, transcendentals=0, bytes_accessed=sum(part.size for part in parts.values()) * 4
        ),
        name="place",
    )(spot, *[in_vmem(part) for part in parts.values()], *[in_hbm(w) for w in keep])


def ring(n, step):
    return [(i, (i + step) % n) for i in range(n)]


def shards(local_params, base_params, momentum):
    decoded = encode(local_params, base_params)

    near = ("zl", "y")
    received = lax.all_to_all(decoded, near, 0, 0, tiled=True)
    partial = jnp.sum(received.astype(jnp.float32), axis=0).astype(jnp.bfloat16)

    one, two, three = [
        lax.ppermute(partial, "zh", [(i, i ^ k) for i in range(4)]).astype(jnp.float32)
        for k in (1, 2, 3)
    ]
    total = (partial.astype(jnp.float32) + one) + (two + three)
    average = (total / 32).astype(jnp.bfloat16)

    gathered = lax.all_to_all(
        jnp.broadcast_to(average[None], (8,) + average.shape), near, 0, 0, tiled=True
    )

    first, second = update_base(gathered, base_params, momentum)
    new_momentum = update_momentum(gathered, momentum)

    def swap(part):
        return lax.ppermute(part, "core", ring(2, 1))

    spot = jnp.stack([lax.axis_index("x"), lax.axis_index("core")]).astype(jnp.int32)
    left = [lax.ppermute(half, "x", ring(4, 1)) for half in (first, second)]
    right = [lax.ppermute(half, "x", ring(4, 3)) for half in (second, first)]
    left[0], new_momentum = after(left[0], new_momentum)
    far = [lax.ppermute(left[0], "x", ring(4, 1)), lax.ppermute(right[0], "x", ring(4, 3))]
    from_left = join(left[0], left[1])
    from_right = join(right[1], right[0])
    new_base = place(
        spot,
        {
            (0, 0, 0): first,
            (0, 0, 1): second,
            (0, 1, 0): swap(first),
            (0, 1, 1): swap(second),
            (3, 0, 0): from_left,
            (1, 0, 0): from_right,
        },
    )
    from_far, new_base = join_after(far[0], far[1], new_base)
    new_base = place(
        spot,
        {
            (3, 1, 0): swap(from_left),
            (1, 1, 0): swap(from_right),
            (2, 0, 0): from_far,
        },
        new_base,
    )
    new_base = place(spot, {(2, 1, 0): swap(from_far)}, new_base)
    return (new_base, new_momentum)


def solution(mesh):
    fine = Mesh(mesh.devices.reshape(4, 2, 4, 4, 2), ("zh", "zl", "y", "x", "core"))
    rep, fsdp = ("zh", "zl", "y"), ("x", "core")
    in_specs = (P(rep, fsdp, None), P(fsdp, None), P(fsdp, None))
    out_specs = (P(), P(fsdp, None))
    return jax.shard_map(shards, mesh=fine, in_specs=in_specs, out_specs=out_specs, check_vma=False)
```

```python
import functools

import jax
import jax.numpy as jnp
from jax import lax
from jax.experimental import pallas as pl
from jax.experimental.pallas import tpu as pltpu
from jax.sharding import Mesh, PartitionSpec as P

BLOCK = 32

floor_value = 0.5
spread_ratio = 3.0
code_peak = 6.0
outer_rate = 0.7
momentum_coef = 0.9

ROWS = 32
HALF = 16
COLS = 8192
PIECES = 4
WIDE = COLS // PIECES
LANES = 128

SMALL = pltpu.CompilerParams(vmem_limit_bytes=8 << 20)
TINY = pltpu.CompilerParams(vmem_limit_bytes=4 << 20)


def encode_kernel(local_hbm, base_hbm, out_ref, local_ref, base_ref, sems):
    copies = []
    for half in range(2):
        rows = pl.ds(half * HALF, HALF)
        copies.append(
            (
                pltpu.make_async_copy(
                    local_hbm.at[0, rows, :], local_ref.at[half], sems.at[0, half]
                ),
                pltpu.make_async_copy(base_hbm.at[rows, :], base_ref.at[half], sems.at[1, half]),
            )
        )
    for pair in copies:
        for copy in pair:
            copy.start()
    block = lax.broadcasted_iota(jnp.int32, (LANES, LANES), 0) // BLOCK
    block_t = lax.broadcasted_iota(jnp.int32, (LANES, LANES), 1) // BLOCK
    same_block = jnp.where(block == block_t, 1.0 / BLOCK, 0.0).astype(jnp.float32)
    for k in range(2 * PIECES):
        half, piece = k // PIECES, k % PIECES
        if piece == 0:
            for copy in copies[half]:
                copy.wait()
        cols = pl.ds(piece * WIDE, WIDE)
        grad = base_ref[half, :, cols].astype(jnp.float32) - local_ref[half, :, cols].astype(
            jnp.float32
        )
        tall = jnp.concatenate(
            [grad[:, i * LANES : (i + 1) * LANES] for i in range(WIDE // LANES)], axis=0
        )
        mean_square = jnp.dot(
            tall * tall,
            same_block,
            precision=lax.Precision.HIGHEST,
            preferred_element_type=jnp.float32,
        )
        floored = jnp.maximum(mean_square, floor_value * floor_value)
        scale = (floored * lax.rsqrt(floored) * (1.0 / spread_ratio)).astype(jnp.bfloat16)
        limit = code_peak * scale.astype(jnp.float32)
        decoded = jnp.clip(tall, -limit, limit).astype(jnp.bfloat16)
        for i in range(WIDE // LANES):
            out_ref[k, :, i * LANES : (i + 1) * LANES] = decoded[i * HALF : (i + 1) * HALF]


def in_vmem(value):
    return pltpu.with_memory_space_constraint(value, pltpu.VMEM)


def in_hbm(value):
    return pltpu.with_memory_space_constraint(value, pltpu.HBM)


def encode(local_params, base_rows):
    halves = (2, HALF, COLS)
    return pl.pallas_call(
        encode_kernel,
        out_shape=pltpu.VMEM((2 * PIECES, HALF, WIDE), jnp.bfloat16),
        in_specs=[pl.BlockSpec(memory_space=pltpu.HBM)] * 2,
        scratch_shapes=[
            pltpu.VMEM(halves, jnp.bfloat16),
            pltpu.VMEM(halves, jnp.bfloat16),
            pltpu.SemaphoreType.DMA((2, 2)),
        ],
        compiler_params=SMALL,
        name="encode",
    )(in_hbm(local_params), in_hbm(base_rows))


def pieces():
    for half in range(2):
        for piece in range(PIECES):
            rows, cols = pl.ds(half * HALF, HALF), pl.ds(piece * WIDE, WIDE)
            yield half, half * PIECES + piece, rows, cols


def step_momentum(average, momentum):
    return momentum_coef * momentum + average


def base_kernel(average_ref, base_ref, momentum_ref, *new_base_refs):
    for half, k, rows, cols in pieces():
        average = average_ref[k].astype(jnp.float32)
        new_momentum = step_momentum(average, momentum_ref[rows, cols])
        new_base_refs[half][:, cols] = (
            base_ref[rows, cols].astype(jnp.float32)
            - outer_rate * (average + momentum_coef * new_momentum)
        ).astype(jnp.bfloat16)


def update_base(average, base_rows, momentum):
    part = pltpu.VMEM((HALF, COLS), jnp.bfloat16)
    return pl.pallas_call(
        base_kernel,
        out_shape=(part, part),
        compiler_params=SMALL,
        name="update_base",
    )(in_vmem(average), base_rows, momentum)


def momentum_kernel(average_ref, momentum_hbm, new_hbm, momentum_ref, new_ref, sems):
    reads, writes = [], []
    for half in range(2):
        rows = pl.ds(half * HALF, HALF)
        reads.append(
            pltpu.make_async_copy(momentum_hbm.at[rows, :], momentum_ref.at[half], sems.at[0, half])
        )
        writes.append(pltpu.make_async_copy(new_ref.at[half], new_hbm.at[rows, :], sems.at[1, half]))
    for copy in reads:
        copy.start()
    for half in range(2):
        reads[half].wait()
        for piece in range(PIECES):
            cols = pl.ds(piece * WIDE, WIDE)
            new_ref[half, :, cols] = step_momentum(
                average_ref[half * PIECES + piece].astype(jnp.float32), momentum_ref[half, :, cols]
            )
        writes[half].start()
    for copy in writes:
        copy.wait()


def update_momentum(average, momentum):
    hbm = pl.BlockSpec(memory_space=pltpu.HBM)
    return pl.pallas_call(
        momentum_kernel,
        out_shape=pltpu.HBM((ROWS, COLS), jnp.float32),
        in_specs=[pl.BlockSpec(memory_space=pltpu.VMEM), hbm],
        out_specs=hbm,
        scratch_shapes=[
            pltpu.VMEM((2, HALF, COLS), jnp.float32),
            pltpu.VMEM((2, HALF, COLS), jnp.float32),
            pltpu.SemaphoreType.DMA((2, 2)),
        ],
        compiler_params=SMALL,
        name="update_momentum",
    )(in_vmem(average), in_hbm(momentum))


def after_kernel(*refs):
    pass


def after(part, ready):
    vmem, hbm = pl.BlockSpec(memory_space=pltpu.VMEM), pl.BlockSpec(memory_space=pltpu.HBM)
    return pl.pallas_call(
        after_kernel,
        out_shape=(pltpu.VMEM(part.shape, part.dtype), pltpu.HBM(ready.shape, ready.dtype)),
        in_specs=[vmem, hbm],
        out_specs=(vmem, hbm),
        input_output_aliases={0: 0, 1: 1},
        compiler_params=TINY,
        name="after",
    )(in_vmem(part), in_hbm(ready))


def join_kernel(one_ref, two_ref, out_ref):
    out_ref[pl.ds(0, HALF), :] = one_ref[...]
    out_ref[pl.ds(HALF, HALF), :] = two_ref[...]


def join(one, two):
    return pl.pallas_call(
        join_kernel,
        out_shape=pltpu.VMEM((ROWS, COLS), jnp.bfloat16),
        compiler_params=TINY,
        name="join",
    )(in_vmem(one), in_vmem(two))


def join_after_kernel(one_ref, two_ref, *refs):
    join_kernel(one_ref, two_ref, refs[len(refs) // 2])


def join_after(one, two, *ready):
    vmem, hbm = pl.BlockSpec(memory_space=pltpu.VMEM), pl.BlockSpec(memory_space=pltpu.HBM)
    count = len(ready)
    return pl.pallas_call(
        join_after_kernel,
        out_shape=(pltpu.VMEM((ROWS, COLS), jnp.bfloat16),)
        + tuple(pltpu.HBM(array.shape, array.dtype) for array in ready),
        in_specs=[vmem, vmem] + [hbm] * count,
        out_specs=(vmem,) + (hbm,) * count,
        input_output_aliases={2 + k: 1 + k for k in range(count)},
        compiler_params=TINY,
        name="join_after",
    )(in_vmem(one), in_vmem(two), *[in_hbm(array) for array in ready])


def place_kernel(steps, spot_ref, *refs):
    parts, out_ref, sems = refs[: len(steps)], refs[-2], refs[-1]
    copies = []
    for k, (ref, (step, other, half)) in enumerate(zip(parts, steps)):
        x, core = spot_ref[0] ^ step, spot_ref[1] ^ other
        start = pl.multiple_of((x * 2 + core) * ROWS + half * HALF, HALF)
        copies.append(
            pltpu.make_async_copy(ref, out_ref.at[pl.ds(start, ref.shape[0]), :], sems.at[k])
        )
    for copy in copies:
        copy.start()
    for copy in copies:
        copy.wait()


def place(spot, parts, whole=None):
    steps, count = tuple(parts), len(parts)
    keep = [] if whole is None else [whole]
    hbm = pl.BlockSpec(memory_space=pltpu.HBM)
    return pl.pallas_call(
        functools.partial(place_kernel, steps),
        out_shape=pltpu.HBM((8 * ROWS, COLS), jnp.bfloat16),
        in_specs=[pl.BlockSpec(memory_space=pltpu.SMEM)]
        + [pl.BlockSpec(memory_space=pltpu.VMEM)] * count
        + [hbm] * len(keep),
        out_specs=hbm,
        scratch_shapes=[pltpu.SemaphoreType.DMA((count,))],
        input_output_aliases={count + 1: 0} if keep else {},
        compiler_params=TINY,
        cost_estimate=pl.CostEstimate(
            flops=0, transcendentals=0, bytes_accessed=sum(part.size for part in parts.values()) * 4
        ),
        name="place",
    )(spot, *[in_vmem(part) for part in parts.values()], *[in_hbm(w) for w in keep])


def pairs(k, n=4):
    return [(i, i ^ k) for i in range(n)]


def shards(local_params, base_params, momentum):
    decoded = encode(local_params, base_params)

    near = ("zl", "y")
    received = lax.all_to_all(decoded, near, 0, 0, tiled=True)
    partial = jnp.sum(received.astype(jnp.float32), axis=0).astype(jnp.bfloat16)

    for k in (1, 3):
        other = lax.ppermute(partial, "zh", pairs(k))
        total = partial.astype(jnp.float32) + other.astype(jnp.float32)
        partial = total.astype(jnp.bfloat16)
    average = (total / 32).astype(jnp.bfloat16)

    gathered = lax.all_to_all(
        jnp.broadcast_to(average[None], (8,) + average.shape), near, 0, 0, tiled=True
    )

    first, second = update_base(gathered, base_params, momentum)
    new_momentum = update_momentum(gathered, momentum)

    def swap(part):
        return lax.ppermute(part, "core", pairs(1, 2))

    spot = jnp.stack([lax.axis_index("x"), lax.axis_index("core")]).astype(jnp.int32)
    left = [lax.ppermute(half, "x", pairs(1)) for half in (first, second)]
    right = [lax.ppermute(half, "x", pairs(3)) for half in (second, first)]
    left[0], new_momentum = after(left[0], new_momentum)
    far = [lax.ppermute(left[0], "x", pairs(3)), lax.ppermute(right[0], "x", pairs(1))]
    from_left = join(left[0], left[1])
    from_right = join(right[1], right[0])
    new_base = place(
        spot,
        {
            (0, 0, 0): first,
            (0, 0, 1): second,
            (0, 1, 0): swap(first),
            (0, 1, 1): swap(second),
            (1, 0, 0): from_left,
            (3, 0, 0): from_right,
        },
    )
    from_far, new_base = join_after(far[0], far[1], new_base)
    new_base = place(
        spot,
        {
            (1, 1, 0): swap(from_left),
            (3, 1, 0): swap(from_right),
            (2, 0, 0): from_far,
        },
        new_base,
    )
    new_base = place(spot, {(2, 1, 0): swap(from_far)}, new_base)
    return (new_base, new_momentum)


def solution(mesh):
    fine = Mesh(mesh.devices.reshape(4, 2, 4, 4, 2), ("zh", "zl", "y", "x", "core"))
    rep, fsdp = ("zh", "zl", "y"), ("x", "core")
    in_specs = (P(rep, fsdp, None), P(fsdp, None), P(fsdp, None))
    out_specs = (P(), P(fsdp, None))
    return jax.shard_map(shards, mesh=fine, in_specs=in_specs, out_specs=out_specs, check_vma=False)
```

```python
import functools

import jax
import jax.numpy as jnp
from jax import lax
from jax.experimental import pallas as pl
from jax.experimental.pallas import tpu as pltpu
from jax.sharding import Mesh, PartitionSpec as P

BLOCK = 32

floor_value = 0.5
spread_ratio = 3.0
code_peak = 6.0
outer_rate = 0.7
momentum_coef = 0.9

ROWS = 32
HALF = 16
COLS = 8192
PIECES = 4
WIDE = COLS // PIECES
LANES = 128

SMALL = pltpu.CompilerParams(vmem_limit_bytes=8 << 20)
TINY = pltpu.CompilerParams(vmem_limit_bytes=4 << 20)


def encode_kernel(local_hbm, base_hbm, out_ref, local_ref, base_ref, sems):
    copies = []
    for half in range(2):
        rows = pl.ds(half * HALF, HALF)
        copies.append(
            (
                pltpu.make_async_copy(
                    local_hbm.at[0, rows, :], local_ref.at[half], sems.at[0, half]
                ),
                pltpu.make_async_copy(base_hbm.at[rows, :], base_ref.at[half], sems.at[1, half]),
            )
        )
    for pair in copies:
        for copy in pair:
            copy.start()
    block = lax.broadcasted_iota(jnp.int32, (LANES, LANES), 0) // BLOCK
    block_t = lax.broadcasted_iota(jnp.int32, (LANES, LANES), 1) // BLOCK
    same_block = jnp.where(block == block_t, 1.0 / BLOCK, 0.0).astype(jnp.bfloat16)
    for k in range(2 * PIECES):
        half, piece = k // PIECES, k % PIECES
        if piece == 0:
            for copy in copies[half]:
                copy.wait()
        cols = pl.ds(piece * WIDE, WIDE)
        grad = base_ref[half, :, cols].astype(jnp.float32) - local_ref[half, :, cols].astype(
            jnp.float32
        )
        tall = jnp.concatenate(
            [grad[:, i * LANES : (i + 1) * LANES] for i in range(WIDE // LANES)], axis=0
        )
        rest, mean_square = tall * tall, 0.0
        for _ in range(3):
            part = rest.astype(jnp.bfloat16)
            rest = rest - part.astype(jnp.float32)
            mean_square += jnp.dot(part, same_block, preferred_element_type=jnp.float32)
        floored = jnp.maximum(mean_square, floor_value * floor_value)
        scale = (floored * lax.rsqrt(floored) * (1.0 / spread_ratio)).astype(jnp.bfloat16)
        limit = code_peak * scale.astype(jnp.float32)
        decoded = jnp.clip(tall, -limit, limit).astype(jnp.bfloat16)
        for i in range(WIDE // LANES):
            out_ref[k, :, i * LANES : (i + 1) * LANES] = decoded[i * HALF : (i + 1) * HALF]


def in_vmem(value):
    return pltpu.with_memory_space_constraint(value, pltpu.VMEM)


def in_hbm(value):
    return pltpu.with_memory_space_constraint(value, pltpu.HBM)


def encode(local_params, base_rows):
    halves = (2, HALF, COLS)
    return pl.pallas_call(
        encode_kernel,
        out_shape=pltpu.VMEM((2 * PIECES, HALF, WIDE), jnp.bfloat16),
        in_specs=[pl.BlockSpec(memory_space=pltpu.HBM)] * 2,
        scratch_shapes=[
            pltpu.VMEM(halves, jnp.bfloat16),
            pltpu.VMEM(halves, jnp.bfloat16),
            pltpu.SemaphoreType.DMA((2, 2)),
        ],
        compiler_params=SMALL,
        name="encode",
    )(in_hbm(local_params), in_hbm(base_rows))


def pieces():
    for half in range(2):
        for piece in range(PIECES):
            rows, cols = pl.ds(half * HALF, HALF), pl.ds(piece * WIDE, WIDE)
            yield half, half * PIECES + piece, rows, cols


def step_momentum(average, momentum):
    return momentum_coef * momentum + average


def base_kernel(average_ref, base_ref, momentum_ref, *new_base_refs):
    for half, k, rows, cols in pieces():
        average = average_ref[k].astype(jnp.float32)
        new_momentum = step_momentum(average, momentum_ref[rows, cols])
        new_base_refs[half][:, cols] = (
            base_ref[rows, cols].astype(jnp.float32)
            - outer_rate * (average + momentum_coef * new_momentum)
        ).astype(jnp.bfloat16)


def update_base(average, base_rows, momentum):
    part = pltpu.VMEM((HALF, COLS), jnp.bfloat16)
    return pl.pallas_call(
        base_kernel,
        out_shape=(part, part),
        compiler_params=SMALL,
        name="update_base",
    )(in_vmem(average), base_rows, momentum)


def momentum_kernel(average_ref, momentum_hbm, new_hbm, momentum_ref, new_ref, sems):
    reads, writes = [], []
    for part in range(4):
        rows = pl.ds(part * 8, 8)
        reads.append(
            pltpu.make_async_copy(momentum_hbm.at[rows, :], momentum_ref.at[part], sems.at[0, part])
        )
        writes.append(pltpu.make_async_copy(new_ref.at[part], new_hbm.at[rows, :], sems.at[1, part]))
    for copy in reads:
        copy.start()
    for part in range(4):
        reads[part].wait()
        for piece in range(PIECES):
            cols = pl.ds(piece * WIDE, WIDE)
            average = average_ref[part // 2 * PIECES + piece].astype(jnp.float32)
            new_ref[part, :, cols] = step_momentum(
                average[part % 2 * 8 : part % 2 * 8 + 8], momentum_ref[part, :, cols]
            )
        writes[part].start()
    for copy in writes:
        copy.wait()


def update_momentum(average, momentum):
    hbm = pl.BlockSpec(memory_space=pltpu.HBM)
    return pl.pallas_call(
        momentum_kernel,
        out_shape=pltpu.HBM((ROWS, COLS), jnp.float32),
        in_specs=[pl.BlockSpec(memory_space=pltpu.VMEM), hbm],
        out_specs=hbm,
        scratch_shapes=[
            pltpu.VMEM((4, 8, COLS), jnp.float32),
            pltpu.VMEM((4, 8, COLS), jnp.float32),
            pltpu.SemaphoreType.DMA((2, 4)),
        ],
        compiler_params=SMALL,
        name="update_momentum",
    )(in_vmem(average), in_hbm(momentum))


def after_kernel(*refs):
    pass


def after(part, ready):
    vmem, hbm = pl.BlockSpec(memory_space=pltpu.VMEM), pl.BlockSpec(memory_space=pltpu.HBM)
    return pl.pallas_call(
        after_kernel,
        out_shape=(pltpu.VMEM(part.shape, part.dtype), pltpu.HBM(ready.shape, ready.dtype)),
        in_specs=[vmem, hbm],
        out_specs=(vmem, hbm),
        input_output_aliases={0: 0, 1: 1},
        compiler_params=TINY,
        name="after",
    )(in_vmem(part), in_hbm(ready))


def join_kernel(one_ref, two_ref, out_ref):
    out_ref[pl.ds(0, HALF), :] = one_ref[...]
    out_ref[pl.ds(HALF, HALF), :] = two_ref[...]


def join(one, two):
    return pl.pallas_call(
        join_kernel,
        out_shape=pltpu.VMEM((ROWS, COLS), jnp.bfloat16),
        compiler_params=TINY,
        name="join",
    )(in_vmem(one), in_vmem(two))


def join_after_kernel(one_ref, two_ref, *refs):
    join_kernel(one_ref, two_ref, refs[len(refs) // 2])


def join_after(one, two, *ready):
    vmem, hbm = pl.BlockSpec(memory_space=pltpu.VMEM), pl.BlockSpec(memory_space=pltpu.HBM)
    count = len(ready)
    return pl.pallas_call(
        join_after_kernel,
        out_shape=(pltpu.VMEM((ROWS, COLS), jnp.bfloat16),)
        + tuple(pltpu.HBM(array.shape, array.dtype) for array in ready),
        in_specs=[vmem, vmem] + [hbm] * count,
        out_specs=(vmem,) + (hbm,) * count,
        input_output_aliases={2 + k: 1 + k for k in range(count)},
        compiler_params=TINY,
        name="join_after",
    )(in_vmem(one), in_vmem(two), *[in_hbm(array) for array in ready])


def place_kernel(steps, *refs):
    parts, out_ref, sems = refs[: len(steps)], refs[-2], refs[-1]
    own_x, own_core = lax.axis_index("x"), lax.axis_index("core")
    copies = []
    for k, (ref, (step, other, half)) in enumerate(zip(parts, steps)):
        x, core = own_x ^ step, own_core ^ other
        start = pl.multiple_of((x * 2 + core) * ROWS + half * HALF, HALF)
        copies.append(
            pltpu.make_async_copy(ref, out_ref.at[pl.ds(start, ref.shape[0]), :], sems.at[k])
        )
    for copy in copies:
        copy.start()
    for copy in copies:
        copy.wait()


def place(parts, whole=None):
    steps, count = tuple(parts), len(parts)
    keep = [] if whole is None else [whole]
    hbm = pl.BlockSpec(memory_space=pltpu.HBM)
    return pl.pallas_call(
        functools.partial(place_kernel, steps),
        out_shape=pltpu.HBM((8 * ROWS, COLS), jnp.bfloat16),
        in_specs=[pl.BlockSpec(memory_space=pltpu.VMEM)] * count + [hbm] * len(keep),
        out_specs=hbm,
        scratch_shapes=[pltpu.SemaphoreType.DMA((count,))],
        input_output_aliases={count: 0} if keep else {},
        compiler_params=TINY,
        cost_estimate=pl.CostEstimate(
            flops=0, transcendentals=0, bytes_accessed=sum(part.size for part in parts.values()) * 4
        ),
        name="place",
    )(*[in_vmem(part) for part in parts.values()], *[in_hbm(w) for w in keep])


def pairs(k, n=4):
    return [(i, i ^ k) for i in range(n)]


def shards(local_params, base_params, momentum):
    decoded = encode(local_params, base_params)

    near = ("zl", "y")
    received = lax.all_to_all(decoded, near, 0, 0, tiled=True)
    partial = jnp.sum(received.astype(jnp.float32), axis=0).astype(jnp.bfloat16)

    for k in (1, 3):
        other = lax.ppermute(partial, "zh", pairs(k))
        total = partial.astype(jnp.float32) + other.astype(jnp.float32)
        partial = total.astype(jnp.bfloat16)
    average = (total / 32).astype(jnp.bfloat16)

    gathered = lax.all_to_all(
        jnp.broadcast_to(average[None], (8,) + average.shape), near, 0, 0, tiled=True
    )

    first, second = update_base(gathered, base_params, momentum)
    new_momentum = update_momentum(gathered, momentum)

    def swap(part):
        return lax.ppermute(part, "core", pairs(1, 2))

    left = [lax.ppermute(half, "x", pairs(1)) for half in (first, second)]
    right = [lax.ppermute(half, "x", pairs(3)) for half in (second, first)]
    left[0], new_momentum = after(left[0], new_momentum)
    far = [lax.ppermute(left[0], "x", pairs(3)), lax.ppermute(right[0], "x", pairs(1))]
    from_left = join(left[0], left[1])
    from_right = join(right[1], right[0])
    new_base = place(
        {
            (0, 0, 0): first,
            (0, 0, 1): second,
            (0, 1, 0): swap(first),
            (0, 1, 1): swap(second),
            (1, 0, 0): from_left,
            (3, 0, 0): from_right,
        },
    )
    from_far, new_base = join_after(far[0], far[1], new_base)
    new_base = place(
        {
            (1, 1, 0): swap(from_left),
            (3, 1, 0): swap(from_right),
            (2, 0, 0): from_far,
        },
        new_base,
    )
    new_base = place({(2, 1, 0): swap(from_far)}, new_base)
    return (new_base, new_momentum)


def solution(mesh):
    fine = Mesh(mesh.devices.reshape(4, 2, 4, 4, 2), ("zh", "zl", "y", "x", "core"))
    rep, fsdp = ("zh", "zl", "y"), ("x", "core")
    in_specs = (P(rep, fsdp, None), P(fsdp, None), P(fsdp, None))
    out_specs = (P(), P(fsdp, None))
    return jax.shard_map(shards, mesh=fine, in_specs=in_specs, out_specs=out_specs, check_vma=False)
```

```python
import functools

import jax
import jax.numpy as jnp
from jax import lax
from jax.experimental import pallas as pl
from jax.experimental.pallas import tpu as pltpu
from jax.sharding import Mesh, PartitionSpec as P

BLOCK = 32

floor_value = 0.5
spread_ratio = 3.0
code_peak = 6.0
outer_rate = 0.7
momentum_coef = 0.9

ROWS = 32
HALF = 16
COLS = 8192
PIECES = 4
WIDE = COLS // PIECES
LANES = 128

SMALL = pltpu.CompilerParams(vmem_limit_bytes=8 << 20)
TINY = pltpu.CompilerParams(vmem_limit_bytes=4 << 20)


def encode_kernel(local_hbm, base_hbm, out_ref, local_ref, base_ref, sems):
    copies = []
    for half in range(2):
        rows = pl.ds(half * HALF, HALF)
        copies.append(
            (
                pltpu.make_async_copy(
                    local_hbm.at[0, rows, :], local_ref.at[half], sems.at[0, half]
                ),
                pltpu.make_async_copy(base_hbm.at[rows, :], base_ref.at[half], sems.at[1, half]),
            )
        )
    for pair in copies:
        for copy in pair:
            copy.start()
    block = lax.broadcasted_iota(jnp.int32, (LANES, LANES), 0) // BLOCK
    block_t = lax.broadcasted_iota(jnp.int32, (LANES, LANES), 1) // BLOCK
    same_block = jnp.where(block == block_t, 1.0 / BLOCK, 0.0).astype(jnp.bfloat16)
    for k in range(2 * PIECES):
        half, piece = k // PIECES, k % PIECES
        if piece == 0:
            for copy in copies[half]:
                copy.wait()
        cols = pl.ds(piece * WIDE, WIDE)
        grad = base_ref[half, :, cols].astype(jnp.float32) - local_ref[half, :, cols].astype(
            jnp.float32
        )
        tall = jnp.concatenate(
            [grad[:, i * LANES : (i + 1) * LANES] for i in range(WIDE // LANES)], axis=0
        )
        rest, mean_square = tall * tall, 0.0
        for _ in range(3):
            part = rest.astype(jnp.bfloat16)
            rest = rest - part.astype(jnp.float32)
            mean_square += jnp.dot(part, same_block, preferred_element_type=jnp.float32)
        floored = jnp.maximum(mean_square, floor_value * floor_value)
        scale = (floored * lax.rsqrt(floored) * (1.0 / spread_ratio)).astype(jnp.bfloat16)
        limit = code_peak * scale.astype(jnp.float32)
        decoded = jnp.clip(tall, -limit, limit).astype(jnp.bfloat16)
        for i in range(WIDE // LANES):
            out_ref[k, :, i * LANES : (i + 1) * LANES] = decoded[i * HALF : (i + 1) * HALF]


def in_vmem(value):
    return pltpu.with_memory_space_constraint(value, pltpu.VMEM)


def in_hbm(value):
    return pltpu.with_memory_space_constraint(value, pltpu.HBM)


def encode(local_params, base_rows):
    halves = (2, HALF, COLS)
    return pl.pallas_call(
        encode_kernel,
        out_shape=pltpu.VMEM((2 * PIECES, HALF, WIDE), jnp.bfloat16),
        in_specs=[pl.BlockSpec(memory_space=pltpu.HBM)] * 2,
        scratch_shapes=[
            pltpu.VMEM(halves, jnp.bfloat16),
            pltpu.VMEM(halves, jnp.bfloat16),
            pltpu.SemaphoreType.DMA((2, 2)),
        ],
        compiler_params=SMALL,
        name="encode",
    )(in_hbm(local_params), in_hbm(base_rows))


def pieces():
    for half in range(2):
        for piece in range(PIECES):
            rows, cols = pl.ds(half * HALF, HALF), pl.ds(piece * WIDE, WIDE)
            yield half, half * PIECES + piece, rows, cols


def step_momentum(average, momentum):
    return momentum_coef * momentum + average


def base_kernel(average_ref, base_ref, momentum_ref, *new_base_refs):
    for half, k, rows, cols in pieces():
        average = average_ref[k].astype(jnp.float32)
        new_momentum = step_momentum(average, momentum_ref[rows, cols])
        new_base_refs[half][:, cols] = (
            base_ref[rows, cols].astype(jnp.float32)
            - outer_rate * (average + momentum_coef * new_momentum)
        ).astype(jnp.bfloat16)


def update_base(average, base_rows, momentum):
    part = pltpu.VMEM((HALF, COLS), jnp.bfloat16)
    return pl.pallas_call(
        base_kernel,
        out_shape=(part, part),
        compiler_params=SMALL,
        name="update_base",
    )(in_vmem(average), base_rows, momentum)


def momentum_kernel(average_ref, momentum_hbm, new_hbm, momentum_ref, new_ref, sems):
    reads, writes = [], []
    for part in range(4):
        rows = pl.ds(part * 8, 8)
        reads.append(
            pltpu.make_async_copy(momentum_hbm.at[rows, :], momentum_ref.at[part], sems.at[0, part])
        )
        writes.append(pltpu.make_async_copy(new_ref.at[part], new_hbm.at[rows, :], sems.at[1, part]))
    for copy in reads:
        copy.start()
    for part in range(4):
        reads[part].wait()
        for piece in range(PIECES):
            cols = pl.ds(piece * WIDE, WIDE)
            average = average_ref[part // 2 * PIECES + piece].astype(jnp.float32)
            new_ref[part, :, cols] = step_momentum(
                average[part % 2 * 8 : part % 2 * 8 + 8], momentum_ref[part, :, cols]
            )
        writes[part].start()
    for copy in writes:
        copy.wait()


def update_momentum(average, momentum):
    hbm = pl.BlockSpec(memory_space=pltpu.HBM)
    return pl.pallas_call(
        momentum_kernel,
        out_shape=pltpu.HBM((ROWS, COLS), jnp.float32),
        in_specs=[pl.BlockSpec(memory_space=pltpu.VMEM), hbm],
        out_specs=hbm,
        scratch_shapes=[
            pltpu.VMEM((4, 8, COLS), jnp.float32),
            pltpu.VMEM((4, 8, COLS), jnp.float32),
            pltpu.SemaphoreType.DMA((2, 4)),
        ],
        compiler_params=SMALL,
        name="update_momentum",
    )(in_vmem(average), in_hbm(momentum))


def after_kernel(*refs):
    pass


def after(part, ready):
    vmem, hbm = pl.BlockSpec(memory_space=pltpu.VMEM), pl.BlockSpec(memory_space=pltpu.HBM)
    return pl.pallas_call(
        after_kernel,
        out_shape=(pltpu.VMEM(part.shape, part.dtype), pltpu.HBM(ready.shape, ready.dtype)),
        in_specs=[vmem, hbm],
        out_specs=(vmem, hbm),
        input_output_aliases={0: 0, 1: 1},
        compiler_params=TINY,
        name="after",
    )(in_vmem(part), in_hbm(ready))


def join_kernel(one_ref, two_ref, out_ref):
    out_ref[pl.ds(0, HALF), :] = one_ref[...]
    out_ref[pl.ds(HALF, HALF), :] = two_ref[...]


def join(one, two):
    return pl.pallas_call(
        join_kernel,
        out_shape=pltpu.VMEM((ROWS, COLS), jnp.bfloat16),
        compiler_params=TINY,
        name="join",
    )(in_vmem(one), in_vmem(two))


def join_after_kernel(one_ref, two_ref, *refs):
    join_kernel(one_ref, two_ref, refs[len(refs) // 2])


def join_after(one, two, *ready):
    vmem, hbm = pl.BlockSpec(memory_space=pltpu.VMEM), pl.BlockSpec(memory_space=pltpu.HBM)
    count = len(ready)
    return pl.pallas_call(
        join_after_kernel,
        out_shape=(pltpu.VMEM((ROWS, COLS), jnp.bfloat16),)
        + tuple(pltpu.HBM(array.shape, array.dtype) for array in ready),
        in_specs=[vmem, vmem] + [hbm] * count,
        out_specs=(vmem,) + (hbm,) * count,
        input_output_aliases={2 + k: 1 + k for k in range(count)},
        compiler_params=TINY,
        cost_estimate=pl.CostEstimate(flops=15000000000, transcendentals=0, bytes_accessed=0),
        name="join_after",
    )(in_vmem(one), in_vmem(two), *[in_hbm(array) for array in ready])


def place_kernel(steps, *refs):
    parts, out_ref, sems = refs[: len(steps)], refs[-2], refs[-1]
    own_x, own_core = lax.axis_index("x"), lax.axis_index("core")
    copies = []
    for k, (ref, (step, other, half)) in enumerate(zip(parts, steps)):
        x, core = own_x ^ step, own_core ^ other
        start = pl.multiple_of((x * 2 + core) * ROWS + half * HALF, HALF)
        copies.append(
            pltpu.make_async_copy(ref, out_ref.at[pl.ds(start, ref.shape[0]), :], sems.at[k])
        )
    for copy in copies:
        copy.start()
    for copy in copies:
        copy.wait()


def place(parts, whole=None):
    steps, count = tuple(parts), len(parts)
    keep = [] if whole is None else [whole]
    hbm = pl.BlockSpec(memory_space=pltpu.HBM)
    return pl.pallas_call(
        functools.partial(place_kernel, steps),
        out_shape=pltpu.HBM((8 * ROWS, COLS), jnp.bfloat16),
        in_specs=[pl.BlockSpec(memory_space=pltpu.VMEM)] * count + [hbm] * len(keep),
        out_specs=hbm,
        scratch_shapes=[pltpu.SemaphoreType.DMA((count,))],
        input_output_aliases={count: 0} if keep else {},
        compiler_params=TINY,
        cost_estimate=pl.CostEstimate(flops=0, transcendentals=0, bytes_accessed=0),
        name="place",
    )(*[in_vmem(part) for part in parts.values()], *[in_hbm(w) for w in keep])


def pairs(k, n=4):
    return [(i, i ^ k) for i in range(n)]


def shards(local_params, base_params, momentum):
    decoded = encode(local_params, base_params)

    near = ("zl", "y")
    received = lax.all_to_all(decoded, near, 0, 0, tiled=True)
    partial = jnp.sum(received.astype(jnp.float32), axis=0).astype(jnp.bfloat16)

    for k in (3, 1):
        other = lax.ppermute(partial, "zh", pairs(k))
        total = partial.astype(jnp.float32) + other.astype(jnp.float32)
        partial = total.astype(jnp.bfloat16)
    average = (total / 32).astype(jnp.bfloat16)

    gathered = lax.all_to_all(
        jnp.broadcast_to(average[None], (8,) + average.shape), near, 0, 0, tiled=True
    )

    first, second = update_base(gathered, base_params, momentum)
    new_momentum = update_momentum(gathered, momentum)

    def swap(part):
        return lax.ppermute(part, "core", pairs(1, 2))

    left = [lax.ppermute(half, "x", pairs(1)) for half in (first, second)]
    right = [lax.ppermute(half, "x", pairs(3)) for half in (second, first)]
    left[0], new_momentum = after(left[0], new_momentum)
    far = [lax.ppermute(left[0], "x", pairs(3)), lax.ppermute(right[0], "x", pairs(1))]
    from_left = join(left[0], left[1])
    from_right = join(right[1], right[0])
    new_base = place(
        {
            (0, 0, 0): first,
            (0, 0, 1): second,
            (0, 1, 0): swap(first),
            (0, 1, 1): swap(second),
            (1, 0, 0): from_left,
            (3, 0, 0): from_right,
        },
    )
    from_far, new_base = join_after(far[0], far[1], new_base)
    new_base = place(
        {
            (1, 1, 0): swap(from_left),
            (3, 1, 0): swap(from_right),
            (2, 0, 0): from_far,
        },
        new_base,
    )
    new_base = place({(2, 1, 0): swap(from_far)}, new_base)
    return (new_base, new_momentum)


def solution(mesh):
    fine = Mesh(mesh.devices.reshape(4, 2, 4, 4, 2), ("zh", "zl", "y", "x", "core"))
    rep, fsdp = ("zh", "zl", "y"), ("x", "core")
    in_specs = (P(rep, fsdp, None), P(fsdp, None), P(fsdp, None))
    out_specs = (P(), P(fsdp, None))
    return jax.shard_map(shards, mesh=fine, in_specs=in_specs, out_specs=out_specs, check_vma=False)
```

```python
import functools

import jax
import jax.numpy as jnp
from jax import lax
from jax.experimental import pallas as pl
from jax.experimental.pallas import tpu as pltpu
from jax.sharding import Mesh, PartitionSpec as P

BLOCK = 32

floor_value = 0.5
spread_ratio = 3.0
code_peak = 6.0
outer_rate = 0.7
momentum_coef = 0.9

ROWS = 32
HALF = 16
COLS = 8192
PIECES = 4
WIDE = COLS // PIECES
LANES = 128

SMALL = pltpu.CompilerParams(vmem_limit_bytes=8 << 20)
TINY = pltpu.CompilerParams(vmem_limit_bytes=4 << 20)


def encode_kernel(local_hbm, base_hbm, out_ref, local_ref, base_ref, sems):
    copies = []
    for half in range(2):
        rows = pl.ds(half * HALF, HALF)
        copies.append(
            (
                pltpu.make_async_copy(
                    local_hbm.at[0, rows, :], local_ref.at[half], sems.at[0, half]
                ),
                pltpu.make_async_copy(base_hbm.at[rows, :], base_ref.at[half], sems.at[1, half]),
            )
        )
    for pair in copies:
        for copy in pair:
            copy.start()
    block = lax.broadcasted_iota(jnp.int32, (3 * LANES, LANES), 0) % LANES // BLOCK
    block_t = lax.broadcasted_iota(jnp.int32, (3 * LANES, LANES), 1) // BLOCK
    same_block = jnp.where(block == block_t, 1.0 / BLOCK, 0.0).astype(jnp.bfloat16)
    for k in range(2 * PIECES):
        half, piece = k // PIECES, k % PIECES
        if piece == 0:
            for copy in copies[half]:
                copy.wait()
        cols = pl.ds(piece * WIDE, WIDE)
        grad = base_ref[half, :, cols].astype(jnp.float32) - local_ref[half, :, cols].astype(
            jnp.float32
        )
        tall = jnp.concatenate(
            [grad[:, i * LANES : (i + 1) * LANES] for i in range(WIDE // LANES)], axis=0
        )
        rest, parts = tall * tall, []
        for _ in range(3):
            parts.append(rest.astype(jnp.bfloat16))
            rest = rest - parts[-1].astype(jnp.float32)
        mean_square = jnp.dot(
            jnp.concatenate(parts, axis=1), same_block, preferred_element_type=jnp.float32
        )
        floored = jnp.maximum(mean_square, floor_value * floor_value)
        scale = (floored * lax.rsqrt(floored) * (1.0 / spread_ratio)).astype(jnp.bfloat16)
        limit = code_peak * scale.astype(jnp.float32)
        decoded = jnp.clip(tall, -limit, limit).astype(jnp.bfloat16)
        for i in range(WIDE // LANES):
            out_ref[k, :, i * LANES : (i + 1) * LANES] = decoded[i * HALF : (i + 1) * HALF]


def in_vmem(value):
    return pltpu.with_memory_space_constraint(value, pltpu.VMEM)


def in_hbm(value):
    return pltpu.with_memory_space_constraint(value, pltpu.HBM)


def encode(local_params, base_rows):
    halves = (2, HALF, COLS)
    return pl.pallas_call(
        encode_kernel,
        out_shape=pltpu.VMEM((2 * PIECES, HALF, WIDE), jnp.bfloat16),
        in_specs=[pl.BlockSpec(memory_space=pltpu.HBM)] * 2,
        scratch_shapes=[
            pltpu.VMEM(halves, jnp.bfloat16),
            pltpu.VMEM(halves, jnp.bfloat16),
            pltpu.SemaphoreType.DMA((2, 2)),
        ],
        compiler_params=SMALL,
        name="encode",
    )(in_hbm(local_params), in_hbm(base_rows))


def pieces():
    for half in range(2):
        for piece in range(PIECES):
            rows, cols = pl.ds(half * HALF, HALF), pl.ds(piece * WIDE, WIDE)
            yield half, half * PIECES + piece, rows, cols


def step_momentum(average, momentum):
    return momentum_coef * momentum + average


def base_kernel(average_ref, base_ref, momentum_ref, *new_base_refs):
    for half, k, rows, cols in pieces():
        average = average_ref[k].astype(jnp.float32)
        new_momentum = step_momentum(average, momentum_ref[rows, cols])
        new_base_refs[half][:, cols] = (
            base_ref[rows, cols].astype(jnp.float32)
            - outer_rate * (average + momentum_coef * new_momentum)
        ).astype(jnp.bfloat16)


def update_base(average, base_rows, momentum):
    part = pltpu.VMEM((HALF, COLS), jnp.bfloat16)
    return pl.pallas_call(
        base_kernel,
        out_shape=(part, part),
        compiler_params=SMALL,
        name="update_base",
    )(in_vmem(average), base_rows, momentum)


def momentum_kernel(average_ref, momentum_hbm, new_hbm, momentum_ref, new_ref, sems):
    reads, writes = [], []
    for part in range(4):
        rows = pl.ds(part * 8, 8)
        reads.append(
            pltpu.make_async_copy(momentum_hbm.at[rows, :], momentum_ref.at[part], sems.at[0, part])
        )
        writes.append(pltpu.make_async_copy(new_ref.at[part], new_hbm.at[rows, :], sems.at[1, part]))
    for copy in reads:
        copy.start()
    for part in range(4):
        reads[part].wait()
        for piece in range(PIECES):
            cols = pl.ds(piece * WIDE, WIDE)
            average = average_ref[part // 2 * PIECES + piece].astype(jnp.float32)
            new_ref[part, :, cols] = step_momentum(
                average[part % 2 * 8 : part % 2 * 8 + 8], momentum_ref[part, :, cols]
            )
        writes[part].start()
    for copy in writes:
        copy.wait()


def update_momentum(average, momentum):
    hbm = pl.BlockSpec(memory_space=pltpu.HBM)
    return pl.pallas_call(
        momentum_kernel,
        out_shape=pltpu.HBM((ROWS, COLS), jnp.float32),
        in_specs=[pl.BlockSpec(memory_space=pltpu.VMEM), hbm],
        out_specs=hbm,
        scratch_shapes=[
            pltpu.VMEM((4, 8, COLS), jnp.float32),
            pltpu.VMEM((4, 8, COLS), jnp.float32),
            pltpu.SemaphoreType.DMA((2, 4)),
        ],
        compiler_params=SMALL,
        name="update_momentum",
    )(in_vmem(average), in_hbm(momentum))


def after_kernel(*refs):
    pass


def after(part, ready):
    vmem, hbm = pl.BlockSpec(memory_space=pltpu.VMEM), pl.BlockSpec(memory_space=pltpu.HBM)
    return pl.pallas_call(
        after_kernel,
        out_shape=(pltpu.VMEM(part.shape, part.dtype), pltpu.HBM(ready.shape, ready.dtype)),
        in_specs=[vmem, hbm],
        out_specs=(vmem, hbm),
        input_output_aliases={0: 0, 1: 1},
        compiler_params=TINY,
        name="after",
    )(in_vmem(part), in_hbm(ready))


def join_kernel(one_ref, two_ref, out_ref):
    out_ref[pl.ds(0, HALF), :] = one_ref[...]
    out_ref[pl.ds(HALF, HALF), :] = two_ref[...]


def join(one, two):
    return pl.pallas_call(
        join_kernel,
        out_shape=pltpu.VMEM((ROWS, COLS), jnp.bfloat16),
        compiler_params=TINY,
        name="join",
    )(in_vmem(one), in_vmem(two))


def join_after_kernel(one_ref, two_ref, *refs):
    join_kernel(one_ref, two_ref, refs[len(refs) // 2])


def join_after(one, two, *ready):
    vmem, hbm = pl.BlockSpec(memory_space=pltpu.VMEM), pl.BlockSpec(memory_space=pltpu.HBM)
    count = len(ready)
    return pl.pallas_call(
        join_after_kernel,
        out_shape=(pltpu.VMEM((ROWS, COLS), jnp.bfloat16),)
        + tuple(pltpu.HBM(array.shape, array.dtype) for array in ready),
        in_specs=[vmem, vmem] + [hbm] * count,
        out_specs=(vmem,) + (hbm,) * count,
        input_output_aliases={2 + k: 1 + k for k in range(count)},
        compiler_params=TINY,
        cost_estimate=pl.CostEstimate(flops=15000000000, transcendentals=0, bytes_accessed=0),
        name="join_after",
    )(in_vmem(one), in_vmem(two), *[in_hbm(array) for array in ready])


def place_kernel(steps, *refs):
    parts, out_ref, sems = refs[: len(steps)], refs[-2], refs[-1]
    own_x, own_core = lax.axis_index("x"), lax.axis_index("core")
    copies = []
    for k, (ref, (step, other, half)) in enumerate(zip(parts, steps)):
        x, core = own_x ^ step, own_core ^ other
        start = pl.multiple_of((x * 2 + core) * ROWS + half * HALF, HALF)
        copies.append(
            pltpu.make_async_copy(ref, out_ref.at[pl.ds(start, ref.shape[0]), :], sems.at[k])
        )
    for copy in copies:
        copy.start()
    for copy in copies:
        copy.wait()


def place(parts, whole=None):
    steps, count = tuple(parts), len(parts)
    keep = [] if whole is None else [whole]
    hbm = pl.BlockSpec(memory_space=pltpu.HBM)
    return pl.pallas_call(
        functools.partial(place_kernel, steps),
        out_shape=pltpu.HBM((8 * ROWS, COLS), jnp.bfloat16),
        in_specs=[pl.BlockSpec(memory_space=pltpu.VMEM)] * count + [hbm] * len(keep),
        out_specs=hbm,
        scratch_shapes=[pltpu.SemaphoreType.DMA((count,))],
        input_output_aliases={count: 0} if keep else {},
        compiler_params=TINY,
        cost_estimate=pl.CostEstimate(flops=0, transcendentals=0, bytes_accessed=0),
        name="place",
    )(*[in_vmem(part) for part in parts.values()], *[in_hbm(w) for w in keep])


def pairs(k, n=4):
    return [(i, i ^ k) for i in range(n)]


def shards(local_params, base_params, momentum):
    decoded = encode(local_params, base_params)

    near = ("zl", "y")
    received = lax.all_to_all(decoded, near, 0, 0, tiled=True)
    partial = jnp.sum(received.astype(jnp.float32), axis=0).astype(jnp.bfloat16)

    for k in (3, 1):
        other = lax.ppermute(partial, "zh", pairs(k))
        total = partial.astype(jnp.float32) + other.astype(jnp.float32)
        partial = total.astype(jnp.bfloat16)
    average = (total / 32).astype(jnp.bfloat16)

    gathered = lax.all_to_all(
        jnp.broadcast_to(average[None], (8,) + average.shape), near, 0, 0, tiled=True
    )

    first, second = update_base(gathered, base_params, momentum)
    new_momentum = update_momentum(gathered, momentum)

    def swap(part):
        return lax.ppermute(part, "core", pairs(1, 2))

    left = [lax.ppermute(half, "x", pairs(1)) for half in (first, second)]
    right = [lax.ppermute(half, "x", pairs(3)) for half in (second, first)]
    left[0], new_momentum = after(left[0], new_momentum)
    far = [lax.ppermute(left[0], "x", pairs(3)), lax.ppermute(right[0], "x", pairs(1))]
    from_left = join(left[0], left[1])
    from_right = join(right[1], right[0])
    new_base = place(
        {
            (0, 0, 0): first,
            (0, 0, 1): second,
            (0, 1, 0): swap(first),
            (0, 1, 1): swap(second),
            (1, 0, 0): from_left,
            (3, 0, 0): from_right,
        },
    )
    from_far, new_base = join_after(far[0], far[1], new_base)
    new_base = place(
        {
            (1, 1, 0): swap(from_left),
            (3, 1, 0): swap(from_right),
            (2, 0, 0): from_far,
        },
        new_base,
    )
    new_base = place({(2, 1, 0): swap(from_far)}, new_base)
    return (new_base, new_momentum)


def solution(mesh):
    fine = Mesh(mesh.devices.reshape(4, 2, 4, 4, 2), ("zh", "zl", "y", "x", "core"))
    rep, fsdp = ("zh", "zl", "y"), ("x", "core")
    in_specs = (P(rep, fsdp, None), P(fsdp, None), P(fsdp, None))
    out_specs = (P(), P(fsdp, None))
    return jax.shard_map(shards, mesh=fine, in_specs=in_specs, out_specs=out_specs, check_vma=False)
```
